32 devices in a mesh: grp: 2 (over x), hist: 16 (over z, y, core).
Axes of the slice: x: 2, y: 2, z: 4, core: 2. Of those that a mesh axis runs over, the one named last changes fastest.
Arguments:
- item_ids: int32 [512], P(('grp', 'hist')), parts along dimension 0, may hold values from 0 to 16383
- item_table: bfloat16 [16384, 1024], P('hist'), may hold values from -6 to 6
- key_cache: bfloat16 [32768, 1024], P(('grp', 'hist')), parts along dimension 0, may hold values from -6 to 6
- value_cache: bfloat16 [32768, 1024], P(('grp', 'hist')), parts along dimension 0, may hold values from -6 to 6
- time_buckets: int32 [32768], P(('grp', 'hist')), parts along dimension 0, may hold values from 0 to 127
- window_start: int32 [2], P('grp'), parts along dimension 0, may hold values from 0 to 16384
- norm_gain: float32 [1024], replicated, may hold values from 0.25 to 1.75
- proj_in: bfloat16 [1024, 2048], replicated, may hold values from -0.1875 to 0.1875
- time_bias: float32 [16, 128], replicated, may hold values from -3 to 3
- pos_bias: float32 [16, 18], replicated, may hold values from -1 to 1
- out_gain: float32 [1024], replicated, may hold values from 0.25 to 1.75
- proj_out: bfloat16 [1024, 1024], replicated, may hold values from -0.1875 to 0.1875
Outputs:
- scored: bfloat16 [512, 1024], P(('grp', 'hist')), parts along dimension 0
The draws below stay inside these ranges and needn't reach their ends.
There are 2 independent parts, one for each index of `grp`. The reference program is written for one: setup_inputs(seed, part) draws one part's arguments, and reference() takes and returns one part's arrays. A program takes and returns all parts, laid end to end along the dimension named above; an argument that names none is the same for every part. Nothing has to cross between parts.
All inputs are finite; a program needn't handle non-finite values.
Results may differ from the reference program's by a relative error of at most 0.0075.
Values may be sent and summed in bfloat16 or wider, within the bound.
A program may use at most 128 MiB of HBM per device.

```python
import jax
import jax.numpy as jnp
from jax import lax

D = 1024
HEADS = 16
HEAD_DIM = 64
NTB = 128
NPOS = 18
EV_DEV = 1024
CANDS = 256
WINDOW = 16384
HISTORY = 32768
ITEMS = 16384
N_HIST = 16


def place_ends(array, rng, smallest, high):
    place = [jax.random.randint(jax.random.fold_in(rng, axis), (), 0, length) for axis, length in enumerate(array.shape)]
    widest = array.shape.index(max(array.shape))
    neighbour = place[:widest] + [(place[widest] + 1) % array.shape[widest]] + place[widest + 1:]
    return array.at[tuple(place)].set(smallest).at[tuple(neighbour)].set(high)


def block_levels(key, dims, split, smallest, top_value):
    gain = 1.0
    for position, parts in split:
        heights = jax.random.uniform(jax.random.fold_in(jax.random.fold_in(key, 6), position), (parts,), jnp.float32, smallest / len(split), top_value / len(split))
        gain = gain * jnp.repeat(jnp.exp(heights), dims[position] // parts).reshape((-1,) + (1,) * (len(dims) - 1 - position))
    return gain


def noise(own_key, shape, scale, most, cuts=(), held_as=jnp.bfloat16):
    factor_of = block_levels(own_key, shape, cuts, -0.22, 0.18) if cuts else 1.0
    drawn = jax.random.normal(own_key, shape, jnp.float32) * scale * factor_of
    return jnp.minimum(jnp.maximum(drawn, -most), most).astype(held_as)


def setup_inputs(seed: int = 0, part: int = 0) -> dict:
    key_list = jax.random.split(jax.random.key(seed), 13)
    part_keys = jax.random.split(jax.random.fold_in(key_list[12], part), 13)
    return {
        "item_ids": place_ends(jax.random.randint(part_keys[0], (CANDS,), 0, ITEMS), jax.random.fold_in(part_keys[0], 1), 0, ITEMS - 1).astype(jnp.int32),
        "item_table": noise(key_list[1], (ITEMS, D), 1.0, 6.0, ((0, 16),)),
        "key_cache": noise(part_keys[2], (WINDOW, D), 1.0, 6.0, ((0, 16),)),
        "value_cache": noise(part_keys[3], (WINDOW, D), 1.0, 6.0, ((0, 16),)),
        "time_buckets": place_ends(jax.random.randint(part_keys[4], (WINDOW,), 0, NTB), jax.random.fold_in(part_keys[4], 1), 0, NTB - 1).astype(jnp.int32),
        "window_start": jax.random.randint(part_keys[5], (1,), 0, WINDOW + 1).astype(jnp.int32),
        "norm_gain": jnp.clip(1.0 + 0.15 * jax.random.normal(key_list[6], (D,), jnp.float32), 0.25, 1.75),
        "proj_in": noise(key_list[7], (D, 2 * D), D ** -0.5, 0.1875),
        "time_bias": noise(key_list[8], (HEADS, NTB), 0.5, 3.0, (), jnp.float32),
        "pos_bias": jnp.clip(jax.random.uniform(key_list[9], (HEADS, NPOS), jnp.float32, -1.0, 1.0), -1.0, 1.0),
        "out_gain": jnp.clip(1.0 + 0.15 * jax.random.normal(key_list[10], (D,), jnp.float32), 0.25, 1.75),
        "proj_out": noise(key_list[11], (D, D), D ** -0.5, 0.1875),
    }


def reference(item_ids, item_table, key_cache, value_cache, time_buckets, window_start, norm_gain, proj_in, time_bias, pos_bias, out_gain, proj_out):
    embedded = item_table[item_ids]
    xfloat = embedded.astype(jnp.float32)
    meansq = lax.optimization_barrier(jnp.mean(xfloat * xfloat, axis=-1, keepdims=True))
    normed = (xfloat * lax.rsqrt(meansq + 1e-06) * norm_gain).astype(jnp.bfloat16)
    projected = jnp.dot(normed, proj_in, preferred_element_type=jnp.float32)
    queries = jax.nn.silu(projected[:, :D]).astype(jnp.bfloat16)
    gates = jax.nn.silu(projected[:, D:]).astype(jnp.bfloat16)
    positions = jnp.arange(WINDOW, dtype=jnp.int32)
    distance = HISTORY - window_start[0] - positions
    thresholds = jnp.left_shift(jnp.ones((NPOS - 1,), jnp.int32), jnp.arange(1, NPOS, dtype=jnp.int32))
    buckets = lax.optimization_barrier(jnp.sum((distance[:, None] >= thresholds[None, :]).astype(jnp.int32), axis=1)).astype(jnp.int32)
    event_bias = time_bias[:, time_buckets] + pos_bias[:, buckets]
    scale = HEAD_DIM ** (-0.5)
    query_heads = queries.reshape(CANDS, HEADS, HEAD_DIM).astype(jnp.float32)
    key_blocks = key_cache.reshape(N_HIST, EV_DEV, HEADS, HEAD_DIM)
    value_blocks = value_cache.reshape(N_HIST, EV_DEV, HEADS, HEAD_DIM)
    bias_blocks = event_bias.reshape(HEADS, N_HIST, EV_DEV).transpose(1, 0, 2)

    def one_block(total, operands):
        keys, values, biases = operands
        scores = jnp.einsum('chd,jhd->chj', query_heads, keys.astype(jnp.float32)) * scale + biases[None]
        weights = jax.nn.silu(scores).astype(jnp.bfloat16)
        return (total + jnp.einsum('chj,jhd->chd', weights.astype(jnp.float32), values.astype(jnp.float32)), None)
    start = jnp.zeros((CANDS, HEADS, HEAD_DIM), jnp.float32)
    attended, _ = lax.scan(one_block, start, (key_blocks, value_blocks, bias_blocks))
    attended = attended.reshape(CANDS, D)
    centred = attended - lax.optimization_barrier(jnp.mean(attended, axis=-1, keepdims=True))
    variance = lax.optimization_barrier(jnp.mean(centred * centred, axis=-1, keepdims=True))
    gated = (centred * lax.rsqrt(variance + 1e-05) * out_gain * gates.astype(jnp.float32)).astype(jnp.bfloat16)
    return (embedded.astype(jnp.float32) + jnp.dot(gated, proj_out, preferred_element_type=jnp.float32)).astype(jnp.bfloat16)
```

```python
import functools

import jax
import jax.numpy as jnp
from jax import lax
from jax.experimental import pallas as pl
from jax.experimental.pallas import tpu as pltpu
from jax.sharding import PartitionSpec as P

LANES = 128
F32 = jnp.float32
BF16 = jnp.bfloat16


def silu(v):
    half = 0.5 * v
    return half + half * jnp.tanh(half)


def kernel(
    n,
    head_dim,
    group_pairs,
    ids_ref,
    table_hbm,
    key_hbm,
    value_hbm,
    tb_ref,
    start_ref,
    norm_gain_ref,
    win_hbm,
    time_bias_ref,
    pos_bias_ref,
    out_gain_ref,
    wout_hbm,
    o_ref,
    table_v,
    key_v,
    value_v,
    win_v,
    wout_v,
    idbuf,
    epart,
    ecore,
    esum,
    erx,
    efull,
    q,
    bias,
    p,
    prx,
    psum,
    arx,
    load_sem,
    id_s,
    id_r,
    ec_s,
    ec_r,
    ers_s,
    ers_r,
    eag_s,
    eag_r,
    fwd_s,
    fwd_r,
    p_s,
    p_r,
    a_s,
    a_r,
):
    me = lax.axis_index("hist")
    core = lax.rem(me, 2)
    other = 1 - core
    chip = me // 2
    nchip = n // 2
    partner = chip * 2 + other
    rows, width = table_v.shape
    events = key_v.shape[0]
    cpd = erx.shape[1]
    half_rows = nchip * cpd
    heads, ntb = time_bias_ref.shape
    npos = pos_bias_ref.shape[1]
    per = LANES // head_dim

    def remote(src, dst, ssem, rsem, dev):
        return pltpu.make_async_remote_copy(
            src_ref=src,
            dst_ref=dst,
            send_sem=ssem,
            recv_sem=rsem,
            device_id={"hist": dev},
            device_id_type=pl.DeviceIdType.MESH,
        )

    loads = [
        pltpu.make_async_copy(a, b, load_sem.at[i])
        for i, (a, b) in enumerate(
            (
                (table_hbm, table_v),
                (win_hbm, win_v),
                (key_hbm, key_v),
                (value_hbm, value_v),
                (wout_hbm, wout_v),
            )
        )
    ]
    for c in loads:
        c.start()

    barrier = pltpu.get_barrier_semaphore()

    def greet(d, _):
        pl.semaphore_signal(
            barrier,
            inc=1,
            device_id={"hist": lax.rem(me + d, n)},
            device_id_type=pl.DeviceIdType.MESH,
        )
        return 0

    lax.fori_loop(1, n, greet, 0)
    pl.semaphore_wait(barrier, n - 1)

    def send_ids(d, _):
        t = lax.rem(me + d, n)
        remote(ids_ref, idbuf.at[me], id_s.at[t], id_r.at[me], t).start()
        return 0

    lax.fori_loop(1, n, send_ids, 0)
    idbuf[me] = ids_ref[...]

    positions = me * events + lax.broadcasted_iota(jnp.int32, (1, events), 1)
    distance = 2 * events * n - start_ref[0] - positions
    buckets = tb_ref[...]
    onehot_t = jnp.where(
        buckets == lax.broadcasted_iota(jnp.int32, (ntb, events), 0), 1.0, 0.0
    ).astype(BF16)
    rest = time_bias_ref[...]
    time_part = jnp.zeros((heads, events), F32)
    for _ in range(3):
        head = rest.astype(BF16)
        rest = rest - head.astype(F32)
        time_part = time_part + jnp.dot(head, onehot_t, preferred_element_type=F32)
    far = jnp.broadcast_to(distance, (heads, events))
    pos_part = jnp.broadcast_to(pos_bias_ref[:, 0:1], (heads, events))
    for k in range(1, npos):
        pos_part = jnp.where(far >= 2**k, pos_bias_ref[:, k : k + 1], pos_part)
    bias[...] = (0.5 * (time_part + pos_part)).reshape(heads, 1, events)

    def wait_ids(d, _):
        t = lax.rem(me + d, n)
        c = remote(ids_ref, idbuf.at[t], id_s.at[t], id_r.at[t], t)
        c.wait_send()
        c.wait_recv()
        return 0

    lax.fori_loop(1, n, wait_ids, 0)
    loads[0].wait()

    per_vec = LANES // cpd
    nvec = half_rows // LANES
    lane = lax.broadcasted_iota(jnp.int32, (1, LANES), 1)
    table_first = me * rows

    def pick(which):
        for v in range(nvec):
            row = jnp.zeros((1, LANES), jnp.int32)
            for j in range(per_vec):
                holder = (v * per_vec + j) * 2 + which
                row = jnp.where(lane // cpd == j, idbuf[holder], row)
            tall = jnp.transpose(jnp.broadcast_to(row, (LANES, LANES))) - table_first
            cols = lax.broadcasted_iota(jnp.int32, (LANES, LANES), 1)
            hot = jnp.concatenate(
                [
                    jnp.where(tall == cols + k * LANES, 1.0, 0.0).astype(BF16)
                    for k in range(rows // LANES)
                ],
                axis=1,
            )
            got = jnp.dot(hot, table_v[...], preferred_element_type=F32).astype(BF16)
            epart[which, pl.ds(v * per_vec, per_vec)] = got.reshape(per_vec, cpd, width)

    pick(other)
    to_partner = remote(epart.at[other], ecore, ec_s, ec_r, partner)
    to_partner.start()
    pick(core)
    to_partner.wait_recv()
    esum[...] = epart[core] + ecore[...]

    def send_e(d, _):
        t = lax.rem(chip + d, nchip)
        remote(esum.at[t], erx.at[chip], ers_s.at[t], ers_r.at[chip], 2 * t + core).start()
        return 0

    lax.fori_loop(1, nchip, send_e, 0)
    erx[chip] = esum[chip]

    def wait_e(d, _):
        t = lax.rem(chip + d, nchip)
        remote(esum.at[t], erx.at[t], ers_s.at[t], ers_r.at[t], 2 * t + core).wait_recv()
        return 0

    lax.fori_loop(1, nchip, wait_e, 0)
    home = jnp.sum(erx[...].astype(F32), axis=0)
    efull[core, chip] = home.astype(BF16)

    def forward(t):
        return remote(
            efull.at[core, t], efull.at[core, t], fwd_s.at[t], fwd_r.at[t], partner
        )

    def send_g(d, _):
        t = lax.rem(chip + d, nchip)
        mine = efull.at[core, chip]
        remote(mine, mine, eag_s.at[t], eag_r.at[chip], 2 * t + core).start()
        return 0

    lax.fori_loop(1, nchip, send_g, 0)
    forward(chip).start()

    def normed_of(x):
        meansq = jnp.mean(x * x, axis=-1, keepdims=True)
        return (x * lax.rsqrt(meansq + 1e-6) * norm_gain_ref[...]).astype(BF16)

    loads[1].wait()
    gates = silu(
        jnp.dot(normed_of(home), win_v[:, width:], preferred_element_type=F32)
    ).astype(BF16)

    def pass_on(d, _):
        t = lax.rem(chip + d, nchip)
        got = efull.at[core, t]
        remote(got, got, eag_s.at[t], eag_r.at[t], 2 * t + core).wait_recv()
        forward(t).start()
        return 0

    lax.fori_loop(1, nchip, pass_on, 0)

    def query(which):
        x = efull[which].reshape(half_rows, width).astype(F32)
        projected = jnp.dot(normed_of(x), win_v[:, :width], preferred_element_type=F32)
        scaled = silu(projected).astype(BF16) * jnp.asarray(0.5 * head_dim**-0.5, BF16)
        q[which] = scaled

    query(core)

    def wait_f(t, _):
        c = remote(efull.at[other, t], efull.at[other, t], fwd_s.at[t], fwd_r.at[t], partner)
        c.wait_recv()
        return 0

    lax.fori_loop(0, nchip, wait_f, 0)
    query(other)
    loads[2].wait()
    loads[3].wait()

    groups = a_s.shape[0]
    gwidth = group_pairs * LANES
    lane_row = lax.broadcasted_iota(jnp.int32, (1, LANES), 1) // head_dim

    def gcols(g):
        return pl.ds(pl.multiple_of(g * gwidth, gwidth), gwidth)

    def share(g):
        c = gcols(g)
        return remote(p.at[other, :, :, c], prx.at[:, :, c], p_s.at[g], p_r.at[g], partner)

    def finish(g):
        share(g).wait_recv()
        c = gcols(g)
        psum[:, :, c] = (p[core, :, :, c].astype(F32) + prx[:, :, c].astype(F32)).astype(BF16)

        def send_a(d, _):
            t = lax.rem(chip + d, nchip)
            remote(
                psum.at[t, :, c], arx.at[chip, :, c], a_s.at[g, t], a_r.at[g, chip], 2 * t + core
            ).start()
            return 0

        lax.fori_loop(1, nchip, send_a, 0)
        arx[chip, :, c] = psum[chip, :, c]

    def attend(g, _):
        for u in range(group_pairs):
            pair = g * group_pairs + u
            c = pl.ds(pl.multiple_of(pair * LANES, LANES), LANES)
            qp = q[:, :, c].reshape(2 * half_rows, LANES)
            kp = key_v[:, c]
            vp = value_v[:, c]
            out = None
            for h in range(per):
                qm = jnp.where(lane_row == h, qp, jnp.zeros_like(qp))
                s = lax.dot_general(
                    qm, kp, (((1,), (1,)), ((), ())), preferred_element_type=F32
                )
                half = s + bias[pair * per + h]
                w = (half + half * jnp.tanh(half)).astype(BF16)
                o = jnp.dot(w, vp, preferred_element_type=F32)
                out = o if out is None else jnp.where(lane_row == h, o, out)
            p[:, :, :, c] = out.astype(BF16).reshape(2, nchip, cpd, LANES)
        share(g).start()

        @pl.when(g >= 1)
        def _():
            finish(g - 1)

        return 0

    lax.fori_loop(0, groups, attend, 0)
    finish(groups - 1)
    loads[4].wait()

    def wait_a(g, _):
        c = gcols(g)

        def inner(d, _):
            t = lax.rem(chip + d, nchip)
            remote(
                psum.at[t, :, c], arx.at[t, :, c], a_s.at[g, t], a_r.at[g, t], 2 * t + core
            ).wait_recv()
            return 0

        lax.fori_loop(1, nchip, inner, 0)
        return 0

    lax.fori_loop(0, groups, wait_a, 0)

    attended = jnp.sum(arx[...].astype(F32), axis=0)
    centred = attended - jnp.mean(attended, axis=-1, keepdims=True)
    variance = jnp.mean(centred * centred, axis=-1, keepdims=True)
    gated = (
        centred * lax.rsqrt(variance + 1e-5) * out_gain_ref[...] * gates.astype(F32)
    ).astype(BF16)
    o_ref[...] = (home + jnp.dot(gated, wout_v[...], preferred_element_type=F32)).astype(BF16)

    to_partner.wait_send()

    def drain(d, _):
        t = lax.rem(chip + d, nchip)
        remote(esum.at[t], erx.at[t], ers_s.at[t], ers_r.at[t], 2 * t + core).wait_send()
        got = efull.at[core, t]
        remote(got, got, eag_s.at[t], eag_r.at[t], 2 * t + core).wait_send()
        forward(t).wait_send()
        return 0

    lax.fori_loop(1, nchip, drain, 0)
    forward(chip).wait_send()

    def drain_a(g, _):
        c = gcols(g)
        share(g).wait_send()

        def inner(d, _):
            t = lax.rem(chip + d, nchip)
            remote(
                psum.at[t, :, c], arx.at[t, :, c], a_s.at[g, t], a_r.at[g, t], 2 * t + core
            ).wait_send()
            return 0

        lax.fori_loop(1, nchip, inner, 0)
        return 0

    lax.fori_loop(0, groups, drain_a, 0)


def on_device(
    n,
    item_ids,
    item_table,
    key_cache,
    value_cache,
    time_buckets,
    window_start,
    norm_gain,
    proj_in,
    time_bias,
    pos_bias,
    out_gain,
    proj_out,
):
    cpd = item_ids.shape[0]
    rows, width = item_table.shape
    events = key_cache.shape[0]
    heads = time_bias.shape[0]
    nchip = n // 2
    half_rows = nchip * cpd
    group_pairs = 2
    groups = width // (group_pairs * LANES)
    dma = pltpu.SemaphoreType.DMA
    vmem = pl.BlockSpec(memory_space=pltpu.VMEM)
    smem = pl.BlockSpec(memory_space=pltpu.SMEM)
    hbm = pl.BlockSpec(memory_space=pl.ANY)
    ids = jnp.tile(item_ids, LANES // cpd)[None, :]
    return pl.pallas_call(
        functools.partial(kernel, n, width // heads, group_pairs),
        out_shape=jax.ShapeDtypeStruct((cpd, width), BF16),
        in_specs=[vmem, hbm, hbm, hbm, vmem, smem, vmem, hbm, vmem, vmem, vmem, hbm],
        out_specs=vmem,
        scratch_shapes=[
            pltpu.VMEM((rows, width), BF16),
            pltpu.VMEM((events, width), BF16),
            pltpu.VMEM((events, width), BF16),
            pltpu.VMEM(proj_in.shape, BF16),
            pltpu.VMEM(proj_out.shape, BF16),
            pltpu.VMEM((n, 1, LANES), jnp.int32),
            pltpu.VMEM((2, nchip, cpd, width), BF16),
            pltpu.VMEM((nchip, cpd, width), BF16),
            pltpu.VMEM((nchip, cpd, width), BF16),
            pltpu.VMEM((nchip, cpd, width), BF16),
            pltpu.VMEM((2, nchip, cpd, width), BF16),
            pltpu.VMEM((2, half_rows, width), BF16),
            pltpu.VMEM((heads, 1, events), F32),
            pltpu.VMEM((2, nchip, cpd, width), BF16),
            pltpu.VMEM((nchip, cpd, width), BF16),
            pltpu.VMEM((nchip, cpd, width), BF16),
            pltpu.VMEM((nchip, cpd, width), BF16),
            dma((5,)),
            dma((n,)),
            dma((n,)),
            dma,
            dma,
            dma((nchip,)),
            dma((nchip,)),
            dma((nchip,)),
            dma((nchip,)),
            dma((nchip,)),
            dma((nchip,)),
            dma((groups,)),
            dma((groups,)),
            dma((groups, nchip)),
            dma((groups, nchip)),
        ],
        compiler_params=pltpu.CompilerParams(
            collective_id=0, has_side_effects=True, vmem_limit_bytes=56 * 1024 * 1024
        ),
    )(
        ids,
        item_table,
        key_cache,
        value_cache,
        time_buckets[None, :],
        window_start,
        norm_gain[None, :],
        proj_in,
        time_bias,
        pos_bias,
        out_gain[None, :],
        proj_out,
    )


def solution(mesh):
    placed = (
        P(("grp", "hist")),
        P("hist", None),
        P(("grp", "hist"), None),
        P(("grp", "hist"), None),
        P(("grp", "hist")),
        P("grp"),
        P(),
        P(),
        P(),
        P(),
        P(),
        P(),
    )
    return jax.shard_map(
        functools.partial(on_device, mesh.shape["hist"]),
        mesh=mesh,
        in_specs=placed,
        out_specs=P(("grp", "hist"), None),
        check_vma=False,
    )
```

```python
import functools

import jax
import jax.numpy as jnp
from jax import lax
from jax.experimental import pallas as pl
from jax.experimental.pallas import tpu as pltpu
from jax.sharding import PartitionSpec as P

LANES = 128
F32 = jnp.float32
BF16 = jnp.bfloat16


def silu(v):
    half = 0.5 * v
    return half + half * jnp.tanh(half)


def kernel(
    n,
    head_dim,
    group_pairs,
    ids_ref,
    table_hbm,
    key_hbm,
    value_hbm,
    tb_ref,
    start_ref,
    norm_gain_ref,
    win_hbm,
    time_bias_ref,
    pos_bias_ref,
    out_gain_ref,
    wout_hbm,
    o_ref,
    table_v,
    key_v,
    value_v,
    win_v,
    wout_v,
    idrow,
    idbuf,
    epart,
    ecore,
    esum,
    erx,
    efull,
    q,
    bias,
    p,
    prx,
    psum,
    arx,
    load_sem,
    id_s,
    id_r,
    ec_s,
    ec_r,
    ers_s,
    ers_r,
    eag_s,
    eag_r,
    fwd_s,
    fwd_r,
    p_s,
    p_r,
    a_s,
    a_r,
):
    me = lax.axis_index("hist")
    core = lax.rem(me, 2)
    other = 1 - core
    chip = me // 2
    nchip = n // 2
    partner = chip * 2 + other
    rows, width = table_v.shape
    events = key_v.shape[0]
    cpd = erx.shape[1]
    half_rows = nchip * cpd
    heads, ntb = time_bias_ref.shape
    npos = pos_bias_ref.shape[1]
    per = LANES // head_dim

    def remote(src, dst, ssem, rsem, dev):
        return pltpu.make_async_remote_copy(
            src_ref=src,
            dst_ref=dst,
            send_sem=ssem,
            recv_sem=rsem,
            device_id={"hist": dev},
            device_id_type=pl.DeviceIdType.MESH,
        )

    loads = [
        pltpu.make_async_copy(a, b, load_sem.at[i])
        for i, (a, b) in enumerate(
            (
                (table_hbm, table_v),
                (win_hbm, win_v),
                (key_hbm, key_v),
                (value_hbm, value_v),
                (wout_hbm, wout_v),
            )
        )
    ]
    for c in loads:
        c.start()

    idrow[...] = jnp.concatenate([ids_ref[...]] * (LANES // cpd), axis=1)
    barrier = pltpu.get_barrier_semaphore()

    def greet(d, _):
        pl.semaphore_signal(
            barrier,
            inc=1,
            device_id={"hist": lax.rem(me + d, n)},
            device_id_type=pl.DeviceIdType.MESH,
        )
        return 0

    lax.fori_loop(1, n, greet, 0)
    pl.semaphore_wait(barrier, n - 1)

    def send_ids(d, _):
        t = lax.rem(me + d, n)
        remote(idrow, idbuf.at[me], id_s, id_r, t).start()
        return 0

    lax.fori_loop(1, n, send_ids, 0)
    idbuf[me] = idrow[...]

    positions = me * events + lax.broadcasted_iota(jnp.int32, (1, events), 1)
    distance = 2 * events * n - start_ref[0] - positions
    buckets = tb_ref[...]
    onehot_t = jnp.where(
        buckets == lax.broadcasted_iota(jnp.int32, (ntb, events), 0), 1.0, 0.0
    ).astype(BF16)
    rest = time_bias_ref[...]
    time_part = jnp.zeros((heads, events), F32)
    for _ in range(3):
        head = rest.astype(BF16)
        rest = rest - head.astype(F32)
        time_part = time_part + jnp.dot(head, onehot_t, preferred_element_type=F32)
    far = jnp.broadcast_to(distance, (heads, events))
    pos_part = jnp.broadcast_to(pos_bias_ref[:, 0:1], (heads, events))
    for k in range(1, npos):
        pos_part = jnp.where(far >= 2**k, pos_bias_ref[:, k : k + 1], pos_part)
    bias[...] = (0.5 * (time_part + pos_part)).reshape(heads, 1, events)

    every = idbuf.at[pl.ds(0, n - 1)]
    ids_done = remote(every, every, id_s, id_r, partner)
    ids_done.wait_send()
    ids_done.wait_recv()
    loads[0].wait()

    per_vec = LANES // cpd
    nvec = half_rows // LANES
    lane = lax.broadcasted_iota(jnp.int32, (1, LANES), 1)
    table_first = me * rows

    def hot_rows(which):
        hots = []
        for v in range(nvec):
            row = jnp.zeros((1, LANES), jnp.int32)
            for j in range(per_vec):
                holder = (v * per_vec + j) * 2 + which
                row = jnp.where(lane // cpd == j, idbuf[holder], row)
            tall = jnp.transpose(jnp.broadcast_to(row, (LANES, LANES))) - table_first
            cols = lax.broadcasted_iota(jnp.int32, (LANES, LANES), 1)
            hots.append(
                jnp.concatenate(
                    [
                        jnp.where(tall == cols + k * LANES, 1.0, 0.0).astype(BF16)
                        for k in range(rows // LANES)
                    ],
                    axis=1,
                )
            )
        return hots

    nchunk = ec_s.shape[0]
    cwidth = width // nchunk
    chunks = [pl.ds(k * cwidth, cwidth) for k in range(nchunk)]

    def pick(which, hots, c):
        for v, hot in enumerate(hots):
            got = jnp.dot(hot, table_v[:, c], preferred_element_type=F32).astype(BF16)
            epart[which, pl.ds(v * per_vec, per_vec), :, c] = got.reshape(per_vec, cpd, cwidth)

    def to_partner(k):
        c = chunks[k]
        return remote(
            epart.at[other, :, :, c], ecore.at[:, :, c], ec_s.at[k], ec_r.at[k], partner
        )

    def owners(k):
        part = erx.at[pl.ds(0, nchip - 1), :, chunks[k]]
        return remote(part, part, ers_s.at[k], ers_r.at[k], partner)

    def gathered(k):
        part = efull.at[0, pl.ds(0, nchip - 1), :, chunks[k]]
        return remote(part, part, eag_s.at[k], eag_r.at[k], partner)

    def forward(k, which):
        half = efull.at[which, :, :, chunks[k]]
        return remote(half, half, fwd_s.at[k], fwd_r.at[k], partner)

    hots = hot_rows(other)
    for k in range(nchunk):
        pick(other, hots, chunks[k])
        to_partner(k).start()
    hots = hot_rows(core)
    for k in range(nchunk):
        pick(core, hots, chunks[k])
        to_partner(k).wait_recv()
        c = chunks[k]
        esum[:, :, c] = epart[core, :, :, c] + ecore[:, :, c]

        def send_e(d, _, k=k, c=c):
            t = lax.rem(chip + d, nchip)
            remote(
                esum.at[t, :, c], erx.at[chip, :, c], ers_s.at[k], ers_r.at[k], 2 * t + core
            ).start()
            return 0

        lax.fori_loop(1, nchip, send_e, 0)
        erx[chip, :, c] = esum[chip, :, c]

    home_parts = []
    for k in range(nchunk):
        owners(k).wait_recv()
        c = chunks[k]
        home_parts.append(jnp.sum(erx[:, :, c].astype(F32), axis=0))
        efull[core, chip, :, c] = home_parts[-1].astype(BF16)

        def send_g(d, _, k=k, c=c):
            t = lax.rem(chip + d, nchip)
            mine = efull.at[core, chip, :, c]
            remote(mine, mine, eag_s.at[k], eag_r.at[k], 2 * t + core).start()
            return 0

        lax.fori_loop(1, nchip, send_g, 0)
    home = jnp.concatenate(home_parts, axis=1)

    def normed_of(x):
        meansq = jnp.mean(x * x, axis=-1, keepdims=True)
        return (x * lax.rsqrt(meansq + 1e-6) * norm_gain_ref[...]).astype(BF16)

    loads[1].wait()
    gates = silu(
        jnp.dot(normed_of(home), win_v[:, width:], preferred_element_type=F32)
    ).astype(BF16)

    for k in range(nchunk):
        gathered(k).wait_recv()
        forward(k, core).start()

    def query(which):
        x = efull[which].reshape(half_rows, width).astype(F32)
        projected = jnp.dot(normed_of(x), win_v[:, :width], preferred_element_type=F32)
        scaled = silu(projected).astype(BF16) * jnp.asarray(0.5 * head_dim**-0.5, BF16)
        q[which] = scaled

    query(core)
    for k in range(nchunk):
        forward(k, other).wait_recv()
    query(other)
    loads[2].wait()
    loads[3].wait()

    groups = p_r.shape[0]
    gwidth = group_pairs * LANES
    lane_row = lax.broadcasted_iota(jnp.int32, (1, LANES), 1) // head_dim

    def gcols(g):
        return pl.ds(pl.multiple_of(g * gwidth, gwidth), gwidth)

    def share(g):
        c = gcols(g)
        return remote(p.at[other, :, :, c], prx.at[:, :, c], p_s, p_r.at[g], partner)

    def finish(g):
        share(g).wait_recv()
        c = gcols(g)
        psum[:, :, c] = (p[core, :, :, c].astype(F32) + prx[:, :, c].astype(F32)).astype(BF16)

        def send_a(d, _):
            t = lax.rem(chip + d, nchip)
            remote(
                psum.at[t, :, c], arx.at[chip, :, c], a_s, a_r, 2 * t + core
            ).start()
            return 0

        lax.fori_loop(1, nchip, send_a, 0)
        arx[chip, :, c] = psum[chip, :, c]

    def attend(g, _):
        for u in range(group_pairs):
            pair = g * group_pairs + u
            c = pl.ds(pl.multiple_of(pair * LANES, LANES), LANES)
            qp = q[:, :, c].reshape(2 * half_rows, LANES)
            kp = key_v[:, c]
            vp = value_v[:, c]
            out = None
            for h in range(per):
                qm = jnp.where(lane_row == h, qp, jnp.zeros_like(qp))
                s = lax.dot_general(
                    qm, kp, (((1,), (1,)), ((), ())), preferred_element_type=F32
                )
                half = s + bias[pair * per + h]
                w = (half + half * jnp.tanh(half)).astype(BF16)
                o = jnp.dot(w, vp, preferred_element_type=F32)
                out = o if out is None else jnp.where(lane_row == h, o, out)
            p[:, :, :, c] = out.astype(BF16).reshape(2, nchip, cpd, LANES)
        share(g).start()

        @pl.when(g >= 1)
        def _():
            finish(g - 1)

        return 0

    lax.fori_loop(0, groups, attend, 0)
    finish(groups - 1)
    loads[4].wait()

    whole = arx.at[pl.ds(0, nchip - 1)]
    sums = remote(whole, whole, a_s, a_r, partner)
    sums.wait_recv()

    attended = jnp.sum(arx[...].astype(F32), axis=0)
    centred = attended - jnp.mean(attended, axis=-1, keepdims=True)
    variance = jnp.mean(centred * centred, axis=-1, keepdims=True)
    gated = (
        centred * lax.rsqrt(variance + 1e-5) * out_gain_ref[...] * gates.astype(F32)
    ).astype(BF16)
    o_ref[...] = (home + jnp.dot(gated, wout_v[...], preferred_element_type=F32)).astype(BF16)

    for k in range(nchunk):
        to_partner(k).wait_send()
        owners(k).wait_send()
        gathered(k).wait_send()
        forward(k, core).wait_send()
    remote(prx, prx, p_s, p_r.at[0], partner).wait_send()
    sums.wait_send()


def on_device(
    n,
    item_ids,
    item_table,
    key_cache,
    value_cache,
    time_buckets,
    window_start,
    norm_gain,
    proj_in,
    time_bias,
    pos_bias,
    out_gain,
    proj_out,
):
    cpd = item_ids.shape[0]
    rows, width = item_table.shape
    events = key_cache.shape[0]
    heads = time_bias.shape[0]
    nchip = n // 2
    half_rows = nchip * cpd
    group_pairs = 2
    nchunk = 2
    groups = width // (group_pairs * LANES)
    dma = pltpu.SemaphoreType.DMA
    vmem = pl.BlockSpec(memory_space=pltpu.VMEM)
    smem = pl.BlockSpec(memory_space=pltpu.SMEM)
    hbm = pl.BlockSpec(memory_space=pl.ANY)
    return pl.pallas_call(
        functools.partial(kernel, n, width // heads, group_pairs),
        out_shape=jax.ShapeDtypeStruct((cpd, width), BF16),
        in_specs=[vmem, hbm, hbm, hbm, vmem, smem, vmem, hbm, vmem, vmem, vmem, hbm],
        out_specs=vmem,
        scratch_shapes=[
            pltpu.VMEM((rows, width), BF16),
            pltpu.VMEM((events, width), BF16),
            pltpu.VMEM((events, width), BF16),
            pltpu.VMEM(proj_in.shape, BF16),
            pltpu.VMEM(proj_out.shape, BF16),
            pltpu.VMEM((1, LANES), jnp.int32),
            pltpu.VMEM((n, 1, LANES), jnp.int32),
            pltpu.VMEM((2, nchip, cpd, width), BF16),
            pltpu.VMEM((nchip, cpd, width), BF16),
            pltpu.VMEM((nchip, cpd, width), BF16),
            pltpu.VMEM((nchip, cpd, width), BF16),
            pltpu.VMEM((2, nchip, cpd, width), BF16),
            pltpu.VMEM((2, half_rows, width), BF16),
            pltpu.VMEM((heads, 1, events), F32),
            pltpu.VMEM((2, nchip, cpd, width), BF16),
            pltpu.VMEM((nchip, cpd, width), BF16),
            pltpu.VMEM((nchip, cpd, width), BF16),
            pltpu.VMEM((nchip, cpd, width), BF16),
            dma((5,)),
            dma,
            dma,
            dma((nchunk,)),
            dma((nchunk,)),
            dma((nchunk,)),
            dma((nchunk,)),
            dma((nchunk,)),
            dma((nchunk,)),
            dma((nchunk,)),
            dma((nchunk,)),
            dma,
            dma((groups,)),
            dma,
            dma,
        ],
        compiler_params=pltpu.CompilerParams(
            collective_id=0, has_side_effects=True, vmem_limit_bytes=56 * 1024 * 1024
        ),
    )(
        item_ids[None, :],
        item_table,
        key_cache,
        value_cache,
        time_buckets[None, :],
        window_start,
        norm_gain[None, :],
        proj_in,
        time_bias,
        pos_bias,
        out_gain[None, :],
        proj_out,
    )


def solution(mesh):
    placed = (
        P(("grp", "hist")),
        P("hist", None),
        P(("grp", "hist"), None),
        P(("grp", "hist"), None),
        P(("grp", "hist")),
        P("grp"),
        P(),
        P(),
        P(),
        P(),
        P(),
        P(),
    )
    return jax.shard_map(
        functools.partial(on_device, mesh.shape["hist"]),
        mesh=mesh,
        in_specs=placed,
        out_specs=P(("grp", "hist"), None),
        check_vma=False,
    )
```

```python
import functools

import jax
import jax.numpy as jnp
from jax import lax
from jax.experimental import pallas as pl
from jax.experimental.pallas import tpu as pltpu
from jax.sharding import PartitionSpec as P

LANES = 128
F32 = jnp.float32
BF16 = jnp.bfloat16


def silu(v):
    half = 0.5 * v
    return half + half * jnp.tanh(half)


def kernel(
    n,
    head_dim,
    group_pairs,
    ids_ref,
    table_hbm,
    key_hbm,
    value_hbm,
    tb_ref,
    start_ref,
    norm_gain_ref,
    win_hbm,
    time_bias_ref,
    pos_bias_ref,
    out_gain_ref,
    wout_hbm,
    o_ref,
    table_v,
    key_v,
    value_v,
    win_v,
    wout_v,
    idrow,
    idbuf,
    epart,
    ecore,
    esum,
    erx,
    efull,
    q,
    bias,
    p,
    prx,
    psum,
    arx,
    load_sem,
    id_s,
    id_r,
    ec_s,
    ec_r,
    ers_s,
    ers_r,
    eag_s,
    eag_r,
    fwd_s,
    fwd_r,
    p_s,
    p_r,
    a_s,
    a_r,
):
    me = lax.axis_index("hist")
    core = lax.rem(me, 2)
    other = 1 - core
    chip = me // 2
    nchip = n // 2
    partner = chip * 2 + other
    rows, width = table_v.shape
    events = key_v.shape[0]
    cpd = erx.shape[1]
    half_rows = nchip * cpd
    heads, ntb = time_bias_ref.shape
    npos = pos_bias_ref.shape[1]
    per = LANES // head_dim

    def remote(src, dst, ssem, rsem, dev):
        return pltpu.make_async_remote_copy(
            src_ref=src,
            dst_ref=dst,
            send_sem=ssem,
            recv_sem=rsem,
            device_id={"hist": dev},
            device_id_type=pl.DeviceIdType.MESH,
        )

    loads = [
        pltpu.make_async_copy(a, b, load_sem.at[i])
        for i, (a, b) in enumerate(
            (
                (table_hbm, table_v),
                (win_hbm, win_v),
                (key_hbm, key_v),
                (value_hbm, value_v),
                (wout_hbm, wout_v),
            )
        )
    ]
    for c in loads:
        c.start()

    idrow[...] = jnp.concatenate([ids_ref[...]] * (LANES // cpd), axis=1)
    barrier = pltpu.get_barrier_semaphore()

    def greet(d, _):
        pl.semaphore_signal(
            barrier,
            inc=1,
            device_id={"hist": lax.rem(me + d, n)},
            device_id_type=pl.DeviceIdType.MESH,
        )
        return 0

    lax.fori_loop(1, n, greet, 0)
    positions = me * events + lax.broadcasted_iota(jnp.int32, (1, events), 1)
    distance = 2 * events * n - start_ref[0] - positions
    buckets = tb_ref[...]
    onehot_t = jnp.where(
        buckets == lax.broadcasted_iota(jnp.int32, (ntb, events), 0), 1.0, 0.0
    ).astype(BF16)
    rest = time_bias_ref[...]
    time_part = jnp.zeros((heads, events), F32)
    for _ in range(3):
        head = rest.astype(BF16)
        rest = rest - head.astype(F32)
        time_part = time_part + jnp.dot(head, onehot_t, preferred_element_type=F32)
    far = jnp.broadcast_to(distance, (heads, events))
    pos_part = jnp.broadcast_to(pos_bias_ref[:, 0:1], (heads, events))
    for k in range(1, npos):
        pos_part = jnp.where(far >= 2**k, pos_bias_ref[:, k : k + 1], pos_part)
    bias[...] = (0.5 * (time_part + pos_part)).reshape(heads, 1, events)

    pl.semaphore_wait(barrier, n - 1)

    def send_ids(d, _):
        t = lax.rem(me + d, n)
        remote(idrow, idbuf.at[me], id_s, id_r, t).start()
        return 0

    lax.fori_loop(1, n, send_ids, 0)
    idbuf[me] = idrow[...]

    every = idbuf.at[pl.ds(0, n - 1)]
    ids_done = remote(every, every, id_s, id_r, partner)
    ids_done.wait_send()
    ids_done.wait_recv()
    loads[0].wait()

    per_vec = LANES // cpd
    nvec = half_rows // LANES
    lane = lax.broadcasted_iota(jnp.int32, (1, LANES), 1)
    table_first = me * rows

    def hot_rows(which):
        hots = []
        for v in range(nvec):
            row = jnp.zeros((1, LANES), jnp.int32)
            for j in range(per_vec):
                holder = (v * per_vec + j) * 2 + which
                row = jnp.where(lane // cpd == j, idbuf[holder], row)
            tall = jnp.transpose(jnp.broadcast_to(row, (LANES, LANES))) - table_first
            cols = lax.broadcasted_iota(jnp.int32, (LANES, LANES), 1)
            hots.append(
                jnp.concatenate(
                    [
                        jnp.where(tall == cols + k * LANES, 1.0, 0.0).astype(BF16)
                        for k in range(rows // LANES)
                    ],
                    axis=1,
                )
            )
        return hots

    nchunk = ec_s.shape[0]
    cwidth = width // nchunk
    chunks = [pl.ds(k * cwidth, cwidth) for k in range(nchunk)]

    def pick(which, hots, c):
        for v, hot in enumerate(hots):
            got = jnp.dot(hot, table_v[:, c], preferred_element_type=F32).astype(BF16)
            epart[which, pl.ds(v * per_vec, per_vec), :, c] = got.reshape(per_vec, cpd, cwidth)

    def to_partner(k):
        c = chunks[k]
        return remote(
            epart.at[other, :, :, c], ecore.at[:, :, c], ec_s.at[k], ec_r.at[k], partner
        )

    def owners(k):
        part = erx.at[pl.ds(0, nchip - 1), :, chunks[k]]
        return remote(part, part, ers_s.at[k], ers_r.at[k], partner)

    def gathered(k):
        part = efull.at[0, pl.ds(0, nchip - 1), :, chunks[k]]
        return remote(part, part, eag_s.at[k], eag_r.at[k], partner)

    def forward(k, which):
        half = efull.at[which, :, :, chunks[k]]
        return remote(half, half, fwd_s.at[k], fwd_r.at[k], partner)

    hots = hot_rows(other)
    for k in range(nchunk):
        pick(other, hots, chunks[k])
        to_partner(k).start()
    hots = hot_rows(core)
    for k in range(nchunk):
        pick(core, hots, chunks[k])
        to_partner(k).wait_recv()
        c = chunks[k]
        esum[:, :, c] = epart[core, :, :, c] + ecore[:, :, c]

        def send_e(d, _, k=k, c=c):
            t = lax.rem(chip + d, nchip)
            remote(
                esum.at[t, :, c], erx.at[chip, :, c], ers_s.at[k], ers_r.at[k], 2 * t + core
            ).start()
            return 0

        lax.fori_loop(1, nchip, send_e, 0)
        erx[chip, :, c] = esum[chip, :, c]

    home_parts = []
    for k in range(nchunk):
        owners(k).wait_recv()
        c = chunks[k]
        home_parts.append(jnp.sum(erx[:, :, c].astype(F32), axis=0))
        efull[core, chip, :, c] = home_parts[-1].astype(BF16)

        def send_g(d, _, k=k, c=c):
            t = lax.rem(chip + d, nchip)
            mine = efull.at[core, chip, :, c]
            remote(mine, mine, eag_s.at[k], eag_r.at[k], 2 * t + core).start()
            return 0

        lax.fori_loop(1, nchip, send_g, 0)
    home = jnp.concatenate(home_parts, axis=1)

    def normed_of(x):
        meansq = jnp.mean(x * x, axis=-1, keepdims=True)
        return (x * lax.rsqrt(meansq + 1e-6) * norm_gain_ref[...]).astype(BF16)

    loads[1].wait()
    gates = silu(
        jnp.dot(normed_of(home), win_v[:, width:], preferred_element_type=F32)
    ).astype(BF16)

    for k in range(nchunk):
        gathered(k).wait_recv()
        forward(k, core).start()

    def query(which):
        x = efull[which].reshape(half_rows, width).astype(F32)
        projected = jnp.dot(normed_of(x), win_v[:, :width], preferred_element_type=F32)
        scaled = silu(projected).astype(BF16) * jnp.asarray(0.5 * head_dim**-0.5, BF16)
        q[which] = scaled

    query(core)
    for k in range(nchunk):
        forward(k, other).wait_recv()
    query(other)
    loads[2].wait()
    loads[3].wait()

    groups = p_r.shape[0]
    gwidth = group_pairs * LANES
    lane_row = lax.broadcasted_iota(jnp.int32, (1, LANES), 1) // head_dim

    def gcols(g):
        return pl.ds(pl.multiple_of(g * gwidth, gwidth), gwidth)

    def share(g):
        c = gcols(g)
        return remote(p.at[other, :, :, c], prx.at[:, :, c], p_s, p_r.at[g], partner)

    def finish(g):
        share(g).wait_recv()
        c = gcols(g)
        psum[:, :, c] = (p[core, :, :, c].astype(F32) + prx[:, :, c].astype(F32)).astype(BF16)

        def send_a(d, _):
            t = lax.rem(chip + d, nchip)
            remote(
                psum.at[t, :, c], arx.at[chip, :, c], a_s, a_r, 2 * t + core
            ).start()
            return 0

        lax.fori_loop(1, nchip, send_a, 0)
        arx[chip, :, c] = psum[chip, :, c]

    def attend(g, _):
        for u in range(group_pairs):
            pair = g * group_pairs + u
            c = pl.ds(pl.multiple_of(pair * LANES, LANES), LANES)
            qp = q[:, :, c].reshape(2 * half_rows, LANES)
            kp = key_v[:, c]
            vp = value_v[:, c]
            out = None
            for h in range(per):
                qm = jnp.where(lane_row == h, qp, jnp.zeros_like(qp))
                s = lax.dot_general(
                    qm, kp, (((1,), (1,)), ((), ())), preferred_element_type=F32
                )
                half = s + bias[pair * per + h]
                w = (half + half * jnp.tanh(half)).astype(BF16)
                o = jnp.dot(w, vp, preferred_element_type=F32)
                out = o if out is None else jnp.where(lane_row == h, o, out)
            p[:, :, :, c] = out.astype(BF16).reshape(2, nchip, cpd, LANES)
        share(g).start()

        @pl.when(g >= 1)
        def _():
            finish(g - 1)

        return 0

    lax.fori_loop(0, groups, attend, 0)
    finish(groups - 1)
    loads[4].wait()

    whole = arx.at[pl.ds(0, nchip - 1)]
    sums = remote(whole, whole, a_s, a_r, partner)
    sums.wait_recv()

    attended = jnp.sum(arx[...].astype(F32), axis=0)
    centred = attended - jnp.mean(attended, axis=-1, keepdims=True)
    variance = jnp.mean(centred * centred, axis=-1, keepdims=True)
    gated = (
        centred * lax.rsqrt(variance + 1e-5) * out_gain_ref[...] * gates.astype(F32)
    ).astype(BF16)
    o_ref[...] = home + jnp.dot(gated, wout_v[...], preferred_element_type=F32)

    for k in range(nchunk):
        to_partner(k).wait_send()
        owners(k).wait_send()
        gathered(k).wait_send()
        forward(k, core).wait_send()
    remote(prx, prx, p_s, p_r.at[0], partner).wait_send()
    sums.wait_send()


def on_device(
    n,
    item_ids,
    item_table,
    key_cache,
    value_cache,
    time_buckets,
    window_start,
    norm_gain,
    proj_in,
    time_bias,
    pos_bias,
    out_gain,
    proj_out,
):
    cpd = item_ids.shape[0]
    rows, width = item_table.shape
    events = key_cache.shape[0]
    heads = time_bias.shape[0]
    nchip = n // 2
    half_rows = nchip * cpd
    group_pairs = 2
    nchunk = 2
    groups = width // (group_pairs * LANES)
    dma = pltpu.SemaphoreType.DMA
    vmem = pl.BlockSpec(memory_space=pltpu.VMEM)
    smem = pl.BlockSpec(memory_space=pltpu.SMEM)
    hbm = pl.BlockSpec(memory_space=pl.ANY)
    return pl.pallas_call(
        functools.partial(kernel, n, width // heads, group_pairs),
        out_shape=jax.ShapeDtypeStruct((cpd, width), F32),
        in_specs=[vmem, hbm, hbm, hbm, vmem, smem, vmem, hbm, vmem, vmem, vmem, hbm],
        out_specs=vmem,
        scratch_shapes=[
            pltpu.VMEM((rows, width), BF16),
            pltpu.VMEM((events, width), BF16),
            pltpu.VMEM((events, width), BF16),
            pltpu.VMEM(proj_in.shape, BF16),
            pltpu.VMEM(proj_out.shape, BF16),
            pltpu.VMEM((1, LANES), jnp.int32),
            pltpu.VMEM((n, 1, LANES), jnp.int32),
            pltpu.VMEM((2, nchip, cpd, width), BF16),
            pltpu.VMEM((nchip, cpd, width), BF16),
            pltpu.VMEM((nchip, cpd, width), BF16),
            pltpu.VMEM((nchip, cpd, width), BF16),
            pltpu.VMEM((2, nchip, cpd, width), BF16),
            pltpu.VMEM((2, half_rows, width), BF16),
            pltpu.VMEM((heads, 1, events), F32),
            pltpu.VMEM((2, nchip, cpd, width), BF16),
            pltpu.VMEM((nchip, cpd, width), BF16),
            pltpu.VMEM((nchip, cpd, width), BF16),
            pltpu.VMEM((nchip, cpd, width), BF16),
            dma((5,)),
            dma,
            dma,
            dma((nchunk,)),
            dma((nchunk,)),
            dma((nchunk,)),
            dma((nchunk,)),
            dma((nchunk,)),
            dma((nchunk,)),
            dma((nchunk,)),
            dma((nchunk,)),
            dma,
            dma((groups,)),
            dma,
            dma,
        ],
        compiler_params=pltpu.CompilerParams(
            collective_id=0, has_side_effects=True, vmem_limit_bytes=56 * 1024 * 1024
        ),
    )(
        item_ids[None, :],
        item_table,
        key_cache,
        value_cache,
        time_buckets[None, :],
        window_start,
        norm_gain[None, :],
        proj_in,
        time_bias,
        pos_bias,
        out_gain[None, :],
        proj_out,
    ).astype(BF16)


def solution(mesh):
    placed = (
        P(("grp", "hist")),
        P("hist", None),
        P(("grp", "hist"), None),
        P(("grp", "hist"), None),
        P(("grp", "hist")),
        P("grp"),
        P(),
        P(),
        P(),
        P(),
        P(),
        P(),
    )
    return jax.shard_map(
        functools.partial(on_device, mesh.shape["hist"]),
        mesh=mesh,
        in_specs=placed,
        out_specs=P(("grp", "hist"), None),
        check_vma=False,
    )
```
